128 devices in a mesh: section: 8 (over y_lo, x), expert: 16 (over y_hi, z, core).
Axes of the slice: x: 4, y: 4 (y_hi: 2, y_lo: 2; y = y_hi * 2 + y_lo), z: 4, core: 2. Of those that a mesh axis runs over, the one named last changes fastest.
Arguments:
- tokens: bfloat16 [2, 8, 1024, 7168], P(None, 'section', 'expert'), may hold values from -6 to 6
- route_ids: int32 [2, 8, 1024, 2], P(None, 'section', 'expert'), may hold values from 0 to 3, as said below
- slot_index: int32 [2, 8, 1024, 2], P(None, 'section', 'expert'), may hold values from 0 to 32, as said below
- gate_values: float32 [2, 8, 1024, 2], P(None, 'section', 'expert'), may hold values from 0.2 to 1
- w_gate: bfloat16 [8, 16, 7168, 512], P('section', 'expert'), may hold values from -0.0625 to 0.0625
- w_up: bfloat16 [8, 16, 7168, 512], P('section', 'expert'), may hold values from -0.0625 to 0.0625
- w_down: bfloat16 [8, 16, 512, 7168], P('section', 'expert'), may hold values from -0.125 to 0.125
Outputs:
- handed: bfloat16 [2, 8, 1024, 7168], P(None, 'section', 'expert')
The draws below stay inside these ranges and needn't reach their ends.
Inputs may be any that keep to these rules, and one draw needn't show every extreme that they name: `route_ids`: each row names 2 different experts. `slot_index`: within the rows of one device of one front and layer, the choices naming one expert are numbered 0, 1, 2, ... in some order; numbers from 32 on are replaced by 32, which marks a dropped choice.
All inputs are finite; a program needn't handle non-finite values.
Results may differ from the reference program's by a relative error of at most 0.015.
Values may be sent and summed in bfloat16 or wider, within the bound.
A program may use at most 256 MiB of HBM per device.

```python
import math
import jax
import jax.numpy as jnp
from jax import lax

D = 7168
FFE = 2048
TILE = 128
WSPLIT = 4
TOPK = 2
TOK_DEV = 64
H_DEV = 512
CAP = 32
LAYERS = 8
N_EXPERT = 16


def routing_tables(key):
    nexp = N_EXPERT // WSPLIT
    first, second, third = jax.random.split(key, 3)
    scores = jax.random.randint(first, (2, LAYERS, N_EXPERT, TOK_DEV, nexp), 0, 1000)
    favored = jax.random.randint(second, (2, LAYERS, N_EXPERT, 1, 1), 0, nexp)
    experts_row = jnp.arange(nexp, dtype=jnp.int32)
    scores = scores + 700 * (experts_row == favored).astype(jnp.int32)
    scores = scores * nexp + experts_row
    picked = lax.top_k(scores, TOPK)[1].astype(jnp.int32)
    ehot = (picked[..., None] == experts_row).astype(jnp.int32)
    flat = ehot.reshape(2, LAYERS, N_EXPERT, TOK_DEV * TOPK, nexp)
    count = TOK_DEV * TOPK
    priority = jax.random.randint(third, (2, LAYERS, N_EXPERT, count), 0, 1000)
    priority = priority * count + jnp.arange(count, dtype=jnp.int32)
    order = jnp.argsort(priority, axis=-1, stable=True).astype(jnp.int32)
    inverse = jnp.argsort(order, axis=-1, stable=True).astype(jnp.int32)
    permuted = jnp.take_along_axis(flat, order[..., None], axis=3)
    rank_perm = jnp.cumsum(permuted, axis=3) - 1
    rank = jnp.take_along_axis(rank_perm, inverse[..., None], axis=3)
    slot = jnp.sum(rank * flat, axis=-1).reshape(2, LAYERS, N_EXPERT, TOK_DEV, TOPK)
    slot = jnp.where(slot < CAP, slot, CAP).astype(jnp.int32)
    return (picked.reshape(2, LAYERS, N_EXPERT * TOK_DEV, TOPK), slot.reshape(2, LAYERS, N_EXPERT * TOK_DEV, TOPK))


def draw_route_ids(key, part):
    tables = routing_tables(key)
    return tables[0]


def draw_slot_index(key, part):
    tables = routing_tables(key)
    return tables[1]


def level_of(key, shape, cuts, low, top_value):
    loudness = 1.0
    for dim, shards_of in cuts:
        draws = jax.random.uniform(jax.random.fold_in(jax.random.fold_in(key, 6), dim), (shards_of,), jnp.float32, low / len(cuts), top_value / len(cuts))
        loudness = loudness * jnp.repeat(jnp.exp(draws), shape[dim] // shards_of).reshape((-1,) + (1,) * (len(shape) - 1 - dim))
    return loudness


def noise(own_key, extent, spread, bound, cuts=(), kind=jnp.bfloat16):
    level = level_of(own_key, extent, cuts, -0.22, 0.18) if cuts else 1.0
    result = jax.random.normal(own_key, extent, jnp.float32) * spread * level
    return jnp.minimum(jnp.maximum(result, -bound), bound).astype(kind)


def setup_inputs(seed: int = 0) -> dict:
    key_of = jax.random.split(jax.random.key(seed), 8)
    return {
        "tokens": noise(key_of[0], (2, LAYERS, N_EXPERT * TOK_DEV, D), 1.0, 6.0, ((1, 8), (2, 16))),
        "route_ids": draw_route_ids(jax.random.fold_in(key_of[7], 71), 0),
        "slot_index": draw_slot_index(jax.random.fold_in(key_of[7], 71), 0),
        "gate_values": jnp.clip(jnp.exp(math.log(1.0) - 1.609438 * jax.random.uniform(key_of[3], (2, LAYERS, N_EXPERT * TOK_DEV, TOPK), jnp.float32) ** level_of(key_of[3], (2, LAYERS, N_EXPERT * TOK_DEV, TOPK), ((1, 8), (2, 16)), -0.2, 0.2)), 0.2, 1.0),
        "w_gate": noise(key_of[4], (LAYERS, N_EXPERT, D, H_DEV), D ** -0.5, 0.0625, ((0, 8), (1, 16))),
        "w_up": noise(key_of[5], (LAYERS, N_EXPERT, D, H_DEV), D ** -0.5, 0.0625, ((0, 8), (1, 16))),
        "w_down": noise(key_of[6], (LAYERS, N_EXPERT, H_DEV, D), FFE ** -0.5, 0.125, ((0, 8), (1, 16))),
    }


def coarse_grid(values):
    magnitude = jnp.abs(values)
    spacing = jnp.full_like(magnitude, 2.0 ** -9)
    for power in range(-5, 9):
        spacing = jnp.where(magnitude >= 2.0 ** power, 2.0 ** (power - 3), spacing)
    snapped = jnp.minimum(jnp.floor(magnitude / spacing + 0.5) * spacing, 448.0)
    return jnp.where(values < 0, -snapped, snapped)


def section_layer(x, ids, slots, gates, wg, wu, wd):
    nblk = N_EXPERT
    nexp = N_EXPERT // WSPLIT
    xb = x.reshape(2, nblk, TOK_DEV, D).astype(jnp.float32)
    tiles = xb.reshape(2, nblk, TOK_DEV, D // TILE, TILE)
    scale = (jnp.max(jnp.abs(tiles), axis=-1) + 1e-6) / 448.0
    coded = coarse_grid(tiles / scale[..., None]).astype(jnp.bfloat16).reshape(2, nblk, TOK_DEV, D)
    ids = ids.reshape(2, nblk, TOK_DEV, TOPK)
    slots = slots.reshape(2, nblk, TOK_DEV, TOPK)
    gates = gates.reshape(2, nblk, TOK_DEV, TOPK)
    ehot = (ids[..., None] == jnp.arange(nexp, dtype=jnp.int32)).astype(jnp.float32)
    chot = (slots[..., None] == jnp.arange(CAP, dtype=jnp.int32)).astype(jnp.float32)
    sel = jnp.einsum('fbtke,fbtkc->fbect', ehot, chot)
    sent = jnp.einsum('fbect,fbtd->fbecd', sel, coded.astype(jnp.float32)).astype(jnp.bfloat16)
    sent_scale = jnp.einsum('fbect,fbtd->fbecd', sel, scale, precision=lax.Precision.HIGHEST)
    restored = (sent.astype(jnp.float32).reshape(2, nblk, nexp, CAP, D // TILE, TILE) * sent_scale[..., None])
    restored = restored.reshape(2, nblk, nexp, CAP, D).astype(jnp.bfloat16)
    outs = []
    for e in range(nexp):
        rows = restored[:, :, e].reshape(-1, D)
        total = jnp.zeros((rows.shape[0], D), jnp.float32)
        for w in range(WSPLIT):
            idx = e * WSPLIT + w
            gate = jnp.dot(rows, wg[idx], preferred_element_type=jnp.float32)
            up = jnp.dot(rows, wu[idx], preferred_element_type=jnp.float32)
            hidden = (jax.nn.silu(gate) * up).astype(jnp.bfloat16)
            part = jnp.dot(hidden, wd[idx], preferred_element_type=jnp.float32).astype(jnp.bfloat16)
            total = total + part.astype(jnp.float32)
        outs.append(total.reshape(2, nblk, CAP, D))
    expert_out = jnp.stack(outs, axis=2)
    weights = jnp.einsum('fbtke,fbtkc,fbtk->fbect', ehot, chot, gates)
    branch = jnp.einsum('fbect,fbecd->fbtd', weights, expert_out, precision=lax.Precision.HIGHEST)
    return (xb + branch).astype(jnp.bfloat16).reshape(2, nblk * TOK_DEV, D)


def reference(tokens, route_ids, slot_index, gate_values, w_gate, w_up, w_down):
    layer_outs = []
    for section in range(LAYERS):
        layer_outs.append(section_layer(tokens[:, section], route_ids[:, section], slot_index[:, section],
                                      gate_values[:, section], w_gate[section], w_up[section], w_down[section]))
    stacked = jnp.stack(layer_outs, axis=1)
    front_up = jnp.roll(stacked[0], 1, axis=0)
    front_down = jnp.roll(stacked[1], -1, axis=0)
    return jnp.stack([front_up, front_down], axis=0)
```

```python
import jax
import jax.numpy as jnp
from jax import lax
from jax.experimental import pallas as pl
from jax.experimental.pallas import tpu as pltpu
from jax.sharding import PartitionSpec as P

D = 7168
TILE = 128
TOK = 64
CAP = 32
H = 512
CW = 1024
NC = D // CW
HC = 256
KC = 1024
MESH = pl.DeviceIdType.MESH

CORE = 1
PAIR = 2
CROSS = 6
FAR = 8
DIAG = 14
PARTNERS = (CORE, PAIR, CROSS, FAR, DIAG)

BF = jnp.bfloat16
F32 = jnp.float32


def snap(values):
    mag = jnp.abs(values)
    spacing = jnp.full_like(mag, 2.0**-9)
    for power in range(-5, 9):
        spacing = jnp.where(mag >= 2.0**power, 2.0 ** (power - 3), spacing)
    inverse = jnp.full_like(mag, 2.0**9)
    for power in range(-5, 9):
        inverse = jnp.where(mag >= 2.0**power, 2.0 ** (3 - power), inverse)
    snapped = jnp.minimum(jnp.floor(mag * inverse + 0.5) * spacing, 448.0)
    return jnp.where(values < 0, -snapped, snapped)


def kernel(
    tok_hbm, meta, wg, wu, wd, out, wg2, wu2, wd2,
    tokv, rest, rest_p, meta_p,
    xrows, s_x, s_y, s_d,
    wbuf, dbuf, hid,
    loc, g_x, g_y, g_p, keep, g_d, g_t,
    r_x, r_y, r_p, r_d, r_t, fin,
    tok_sem, w_sem, d_sem, wx_s, wx_r, meta_s, meta_r,
    dis_s, dis_r, com_s, com_r, h_s, h_r,
):
    me = lax.axis_index("expert")
    sec = lax.axis_index("section")
    n_sec = lax.axis_size("section")
    up = lax.rem(sec + 1, n_sec)
    down = lax.rem(sec + n_sec - 1, n_sec)
    mine = (me // 8) * 2 + (me // 4) % 2

    def remote(src, dst, ss, rs, mask):
        return pltpu.make_async_remote_copy(
            src_ref=src, dst_ref=dst, send_sem=ss, recv_sem=rs,
            device_id=(sec, me ^ mask), device_id_type=MESH,
        )

    def tok_copy(f):
        return pltpu.make_async_copy(tok_hbm.at[f], tokv.at[f], tok_sem.at[f])

    def w_copies(ci):
        gate_src, up_src = ((wg, wu), (wg2, wu2))[ci // 2]
        cols = pl.ds((ci % 2) * HC, HC)
        slot = ci % 2
        return (
            pltpu.make_async_copy(gate_src.at[:, cols], wbuf.at[slot, 0], w_sem.at[slot, 0]),
            pltpu.make_async_copy(up_src.at[:, cols], wbuf.at[slot, 1], w_sem.at[slot, 1]),
        )

    def d_copies(j):
        slot = lax.rem(j, 2)
        cols = pl.ds(pl.multiple_of(j * CW, CW), CW)
        return (
            pltpu.make_async_copy(wd.at[:, cols], dbuf.at[slot, pl.ds(0, H)], d_sem.at[slot, 0]),
            pltpu.make_async_copy(wd2.at[:, cols], dbuf.at[slot, pl.ds(H, H)], d_sem.at[slot, 1]),
        )

    for f in range(2):
        tok_copy(f).start()
    for cp in w_copies(0):
        cp.start()

    barrier = pltpu.get_barrier_semaphore()
    for mask in PARTNERS:
        pl.semaphore_signal(barrier, inc=1, device_id=(sec, me ^ mask), device_id_type=MESH)
    for other in (up, down):
        pl.semaphore_signal(barrier, inc=1, device_id=(other, me), device_id_type=MESH)
    pl.semaphore_wait(barrier, len(PARTNERS) + 2)

    w_moves = [
        remote(src, dst, wx_s.at[i], wx_r.at[i], CORE)
        for i, (src, dst) in enumerate(((wg, wg2), (wu, wu2), (wd, wd2)))
    ]
    meta_move = remote(meta, meta_p, meta_s, meta_r, PAIR)
    meta_move.start()

    def restore(f):
        tok_copy(f).wait()

        def step(i, carry):
            for k in range(4):
                cols = pl.ds(pl.multiple_of(i * (4 * TILE), 4 * TILE) + k * TILE, TILE)
                t = tokv[f, :, cols].astype(F32)
                scale = (jnp.max(jnp.abs(t), axis=-1, keepdims=True) + 1e-6) / 448.0
                rest[f, :, cols] = (snap(t * (1.0 / scale)) * scale).astype(BF)
            return carry

        lax.fori_loop(0, D // (4 * TILE), step, 0)

    def selection(table, f, rows):
        row = lax.broadcasted_iota(jnp.int32, (rows, TOK), 0)
        code = ((mine ^ (row // CAP)) * (CAP + 1) + row % CAP).astype(F32)
        hit = (table[f, TOK : TOK + 1, :TOK] == code) | (table[f, TOK + 1 : TOK + 2, :TOK] == code)
        return jnp.where(hit, 1.0, 0.0).astype(BF)

    def gating(table, f, cols):
        col = lax.broadcasted_iota(jnp.int32, (TOK, cols), 1)
        code = ((mine ^ (col // CAP)) * (CAP + 1) + col % CAP).astype(F32)
        weight = jnp.where(table[f, :TOK, 0:1] == code, table[f, :TOK, 2:3], 0.0)
        weight = weight + jnp.where(table[f, :TOK, 1:2] == code, table[f, :TOK, 3:4], 0.0)
        high = weight.astype(BF)
        return high, (weight - high.astype(F32)).astype(BF)

    def pick(f, sel, source, targets):
        def step(j, carry):
            cols = pl.ds(pl.multiple_of(j * CW, CW), CW)
            got = jnp.dot(sel, source[f, :, cols], preferred_element_type=F32).astype(BF)
            for i, (ref, first) in enumerate(targets):
                ref[f, first : first + CAP, cols] = got[i * CAP : (i + 1) * CAP]
            return carry

        lax.fori_loop(0, NC, step, 0)

    def dispatch(f, i):
        row = lambda b: pl.ds(b * CAP, CAP)
        src, dst, mask = (
            (rest.at[f], rest_p.at[f], PAIR),
            (s_d.at[f], xrows.at[f, row(6)], DIAG),
            (s_y.at[f, row(0)], xrows.at[f, row(4)], FAR),
            (s_x.at[f, row(0)], xrows.at[f, row(2)], CROSS),
            (s_y.at[f, row(1)], xrows.at[f, row(5)], FAR),
            (s_x.at[f, row(1)], xrows.at[f, row(3)], CROSS),
            (xrows.at[f, row(6)], xrows.at[f, row(7)], PAIR),
        )[i]
        return remote(src, dst, dis_s.at[f, i], dis_r.at[f, i], mask)

    def prepare(f):
        restore(f)

    def send_own(f):
        dispatch(f, 0).start()
        pick(f, selection(meta, f, 4 * CAP), rest, ((xrows, 0), (s_x, 0), (s_y, 0), (s_d, 0)))
        for i in (1, 2, 3):
            dispatch(f, i).start()

    def send_partner(f):
        dispatch(f, 0).wait_recv()
        pick(f, selection(meta_p, f, 3 * CAP), rest_p, ((xrows, CAP), (s_x, CAP), (s_y, CAP)))
        dispatch(f, 4).start()
        dispatch(f, 5).start()
        dispatch(f, 1).wait_recv()
        dispatch(f, 6).start()

    def gate_up(f):
        for ci in range(4):
            for cp in w_copies(ci):
                cp.wait()
            if ci == 1 and f == 0:
                w_moves[0].wait_recv()
                w_moves[1].wait_recv()
            if ci < 3:
                for cp in w_copies(ci + 1):
                    cp.start()
            elif f == 0:
                for cp in w_copies(0):
                    cp.start()

            def step(k, acc):
                rows = pl.ds(pl.multiple_of(k * KC, KC), KC)
                x = xrows[f, :, rows]
                g = jnp.dot(x, wbuf[ci % 2, 0, rows, :], preferred_element_type=F32)
                u = jnp.dot(x, wbuf[ci % 2, 1, rows, :], preferred_element_type=F32)
                return acc[0] + g, acc[1] + u

            zero = jnp.zeros((8 * CAP, HC), F32)
            g, u = lax.fori_loop(0, D // KC, step, (zero, zero))
            hid[f, :, ci * HC : (ci + 1) * HC] = (g / (1.0 + jnp.exp(-g)) * u).astype(BF)

    def combine(f, j, i):
        src, dst, mask = (
            (g_p, r_p, PAIR),
            (g_x, r_x, CROSS),
            (g_y, r_y, FAR),
            (g_d, r_d, DIAG),
            (g_t, r_t, PAIR),
        )[i]
        return remote(src.at[f, j], dst.at[f, j], com_s.at[f, j, i], com_r.at[f, j, i], mask)

    def first(f, j):
        for cp in d_copies(j):
            cp.wait()

        @pl.when(j < NC - 1)
        def _():
            for cp in d_copies(j + 1):
                cp.start()

        q = jnp.dot(hid[f], dbuf[lax.rem(j, 2)], preferred_element_type=F32).astype(BF)
        g_p[f, j] = q[7 * CAP :]
        g_x[f, j] = q[2 * CAP : 4 * CAP]
        g_y[f, j] = q[4 * CAP : 6 * CAP]
        for i in range(3):
            combine(f, j, i).start()
        loc[f, j] = q[: 2 * CAP]
        keep[f, j] = q[6 * CAP : 7 * CAP]

    def gated(weights, parts):
        z = jnp.concatenate(parts, axis=0)
        high, low = weights
        return jnp.dot(high, z, preferred_element_type=F32) + jnp.dot(low, z, preferred_element_type=F32)

    def second(f, j, weights):
        combine(f, j, 0).wait_recv()
        g_d[f, j] = (keep[f, j].astype(F32) + r_p[f, j].astype(F32)).astype(BF)
        combine(f, j, 3).start()
        combine(f, j, 1).wait_recv()
        combine(f, j, 2).wait_recv()
        g_t[f, j] = gated(weights, [loc[f, j, CAP:], r_x[f, j, CAP:], r_y[f, j, CAP:]]).astype(BF)
        combine(f, j, 4).start()

    def handoff(f, j):
        cols = pl.ds(pl.multiple_of(j * CW, CW), CW)
        return pltpu.make_async_remote_copy(
            src_ref=fin.at[f, j], dst_ref=out.at[f, :, cols],
            send_sem=h_s.at[f, j], recv_sem=h_r.at[f, j],
            device_id=((up, down)[f], me), device_id_type=MESH,
        )

    def third(f, j, weights):
        cols = pl.ds(pl.multiple_of(j * CW, CW), CW)
        combine(f, j, 3).wait_recv()
        combine(f, j, 4).wait_recv()
        total = gated(weights, [loc[f, j, :CAP], r_x[f, j, :CAP], r_y[f, j, :CAP], r_d[f, j]])
        total = total + r_t[f, j].astype(F32) + tokv[f, :, cols].astype(F32)
        fin[f, j] = total.astype(BF)
        handoff(f, j).start()

    def loop(body):
        def step(j, carry):
            body(j)
            return carry

        lax.fori_loop(0, NC, step, 0)

    prepare(0)
    send_own(0)
    for move in w_moves:
        move.start()
    prepare(1)
    meta_move.wait_recv()
    send_partner(0)
    send_own(1)
    for i in (2, 3, 4, 5, 6):
        dispatch(0, i).wait_recv()
    gate_up(0)
    w_moves[2].wait_recv()
    for cp in d_copies(0):
        cp.start()
    send_partner(1)
    loop(lambda j: first(0, j))
    for i in (2, 3, 4, 5, 6):
        dispatch(1, i).wait_recv()
    gate_up(1)
    for cp in d_copies(0):
        cp.start()
    theirs0 = gating(meta_p, 0, 3 * CAP)
    theirs1 = gating(meta_p, 1, 3 * CAP)
    own0 = gating(meta, 0, 4 * CAP)
    own1 = gating(meta, 1, 4 * CAP)

    def middle(j):
        first(1, j)
        second(0, j, theirs0)

    loop(middle)

    def late(j):
        third(0, j, own0)
        second(1, j, theirs1)

    loop(late)
    loop(lambda j: third(1, j, own1))

    meta_move.wait_send()
    for move in w_moves:
        move.wait_send()
    for f in range(2):
        for i in range(7):
            dispatch(f, i).wait_send()

        def drain(j):
            for i in range(5):
                combine(f, j, i).wait_send()
            handoff(f, j).wait()

        loop(drain)


def local(tokens, route_ids, slot_index, gate_values, w_gate, w_up, w_down):
    code = (route_ids[:, 0] * (CAP + 1) + slot_index[:, 0]).astype(F32)
    columns = jnp.concatenate([code, gate_values[:, 0]], axis=-1)
    columns = jnp.pad(columns, ((0, 0), (0, 0), (0, 128 - 4)))
    rows = jnp.pad(jnp.swapaxes(code, 1, 2), ((0, 0), (0, 6), (0, 128 - TOK)))
    meta = jnp.concatenate([columns, rows], axis=1)

    hbm = pl.BlockSpec(memory_space=pltpu.HBM)
    vmem = pl.BlockSpec(memory_space=pltpu.VMEM)
    dma = pltpu.SemaphoreType.DMA
    V = pltpu.VMEM
    shapes = ((2, TOK, D), (D, H), (D, H), (H, D))
    out = pl.pallas_call(
        kernel,
        out_shape=[jax.ShapeDtypeStruct(shape, BF) for shape in shapes],
        in_specs=[hbm, vmem, hbm, hbm, hbm],
        out_specs=[hbm] * 4,
        scratch_shapes=[
            V((2, TOK, D), BF), V((2, TOK, D), BF), V((2, TOK, D), BF), V((2, TOK + 8, 128), F32),
            V((2, 8 * CAP, D), BF), V((2, 2 * CAP, D), BF), V((2, 2 * CAP, D), BF), V((2, CAP, D), BF),
            V((2, 2, D, HC), BF), V((2, 2 * H, CW), BF), V((2, 8 * CAP, 2 * H), BF),
            V((2, NC, 2 * CAP, CW), BF), V((2, NC, 2 * CAP, CW), BF), V((2, NC, 2 * CAP, CW), BF),
            V((2, NC, CAP, CW), BF), V((2, NC, CAP, CW), BF), V((2, NC, CAP, CW), BF), V((2, NC, TOK, CW), BF),
            V((2, NC, 2 * CAP, CW), BF), V((2, NC, 2 * CAP, CW), BF),
            V((2, NC, CAP, CW), BF), V((2, NC, CAP, CW), BF), V((2, NC, TOK, CW), BF), V((2, NC, TOK, CW), BF),
            dma((2,)), dma((2, 2)), dma((2, 2)), dma((3,)), dma((3,)), dma, dma,
            dma((2, 7)), dma((2, 7)), dma((2, NC, 5)), dma((2, NC, 5)), dma((2, NC)), dma((2, NC)),
        ],
        compiler_params=pltpu.CompilerParams(
            collective_id=0, has_side_effects=True, vmem_limit_bytes=62 * 2**20
        ),
        name="relay_layer",
    )(tokens[:, 0], meta, w_gate[0, 0], w_up[0, 0], w_down[0, 0])
    return out[0][:, None]


def solution(mesh):
    spread = P(None, "section", "expert", None)
    split = P("section", "expert", None, None)
    return jax.shard_map(
        local,
        mesh=mesh,
        in_specs=(spread,) * 4 + (split,) * 3,
        out_specs=spread,
        check_vma=False,
    )
```

```python
import jax
import jax.numpy as jnp
from jax import lax
from jax.experimental import pallas as pl
from jax.experimental.pallas import tpu as pltpu
from jax.sharding import PartitionSpec as P

D = 7168
TILE = 128
TOK = 64
CAP = 32
H = 512
CW = 1024
NC = D // CW
STEPS = 2 * NC
HC = 256
KC = 1024
LAG = 2
ROW = 4
MESH = pl.DeviceIdType.MESH

CORE = 1
PAIR = 2
CROSS = 6
FAR = 8
DIAG = 14

BF = jnp.bfloat16
F32 = jnp.float32


def coarse(mag):
    lifted = mag * (2.0**20 + 1.0)
    return lifted - (lifted - mag)


def snap(values):
    mag = jnp.abs(values)
    near = coarse(mag)
    mirror = 2.0 * mag - near
    other = coarse(mirror)
    snapped = jnp.where(other == mirror, jnp.maximum(near, other), near)
    fine = jnp.floor(mag * 512.0 + 0.5) * (1.0 / 512.0)
    snapped = jnp.minimum(jnp.where(mag < 2.0**-6, fine, snapped), 448.0)
    return jnp.where(values < 0, -snapped, snapped)


def kernel(
    tok_hbm, ids, slots, gate_in, wg, wu, wd, out, wg2, wu2, wd2,
    tokv, rest, rest_p, meta, meta_p, gates,
    xrows, s_x, s_y, s_d,
    wbuf, dbuf, hid,
    loc, g_x, g_y, g_p, keep, g_d, g_t,
    r_x, r_y, r_p, r_d, r_t, fin,
    tok_sem, w_sem, d_sem, wx_s, wx_r, meta_s, meta_r,
    dis_s, dis_r, com_s, com_r,
):
    me = lax.axis_index("expert")
    sec = lax.axis_index("section")
    n_sec = lax.axis_size("section")
    up = lax.rem(sec + 1, n_sec)
    down = lax.rem(sec + n_sec - 1, n_sec)
    mine = (me // 8) * 2 + (me // 4) % 2

    flip = (lax.rem(sec, ROW) == 0).astype(jnp.int32)
    ends = (flip == 1) | (lax.rem(sec, ROW) == ROW - 1)

    def summed(f):
        return ends & (f == 1 - flip)

    def remote(src, dst, ss, rs, mask, section=sec):
        return pltpu.make_async_remote_copy(
            src_ref=src, dst_ref=dst, send_sem=ss, recv_sem=rs,
            device_id=(section, me ^ mask), device_id_type=MESH,
        )

    def columns(j):
        return pl.ds(pl.multiple_of(j * CW, CW), CW)

    def each(count, body):
        def step(j, carry):
            body(j)
            return carry

        lax.fori_loop(0, count, step, 0)

    def tok_copy(f):
        return pltpu.make_async_copy(tok_hbm.at[f], tokv.at[f], tok_sem.at[f])

    def w_copies(piece):
        gate_src, up_src = ((wg, wu), (wg2, wu2))[piece % 4 // 2]
        cols = pl.ds((piece % 2) * HC, HC)
        slot = piece % 2
        return (
            pltpu.make_async_copy(gate_src.at[:, cols], wbuf.at[slot, 0], w_sem.at[slot, 0]),
            pltpu.make_async_copy(up_src.at[:, cols], wbuf.at[slot, 1], w_sem.at[slot, 1]),
        )

    def d_copies(m):
        slot = lax.rem(m, 2)
        cols = columns(lax.rem(m, NC))
        return (
            pltpu.make_async_copy(wd.at[:, cols], dbuf.at[slot, pl.ds(0, H)], d_sem.at[slot, 0]),
            pltpu.make_async_copy(wd2.at[:, cols], dbuf.at[slot, pl.ds(H, H)], d_sem.at[slot, 1]),
        )

    for f in range(2):
        tok_copy(f).start()
    for cp in w_copies(0):
        cp.start()

    barrier = pltpu.get_barrier_semaphore()
    peers = [(sec, mask) for mask in (CORE, PAIR, CROSS, FAR, DIAG)]
    peers += [(up, 0), (down, 0)]
    for section, mask in peers:
        pl.semaphore_signal(barrier, inc=1, device_id=(section, me ^ mask), device_id_type=MESH)
    pl.semaphore_wait(barrier, len(peers))

    w_moves = [
        remote(src, dst, wx_s.at[i], wx_r.at[i], CORE)
        for i, (src, dst) in enumerate(((wg, wg2), (wu, wu2), (wd, wd2)))
    ]
    meta_move = remote(meta, meta_p, meta_s, meta_r, PAIR)

    def restore(f, j):
        for k in range(CW // TILE):
            cols = pl.ds(pl.multiple_of(j * CW, CW) + k * TILE, TILE)
            t = tokv[f, :, cols].astype(F32)
            scale = (jnp.max(jnp.abs(t), axis=-1, keepdims=True) + 1e-6) / 448.0
            rest[f, :, cols] = (snap(t * (1.0 / scale)) * scale).astype(BF)

    def selection(table, f, rows):
        row = lax.broadcasted_iota(jnp.int32, (rows, TOK), 0)
        code = ((mine ^ (row // CAP)) * (CAP + 1) + row % CAP).astype(F32)
        hit = (table[f, 0:1, :TOK] == code) | (table[f, 1:2, :TOK] == code)
        return jnp.where(hit, 1.0, 0.0).astype(BF)

    def gating(table, f):
        row = lax.broadcasted_iota(jnp.int32, (4 * CAP, 2 * TOK), 0)
        code = ((mine ^ (row // CAP)) * (CAP + 1) + row % CAP).astype(F32)
        weight = jnp.where(table[f, 0:1] == code, table[f, 2:3], 0.0)
        weight = weight + jnp.where(table[f, 1:2] == code, table[f, 3:4], 0.0)
        weight = weight.T[:TOK]
        high = weight.astype(BF)
        return high, (weight - high.astype(F32)).astype(BF)

    def pick(f, j, table, source, targets):
        sel = selection(table, f, len(targets) * CAP)
        cols = columns(j)
        got = jnp.dot(sel, source[f, :, cols], preferred_element_type=F32).astype(BF)
        for i, (ref, row) in enumerate(targets):
            ref[f, row : row + CAP, cols] = got[i * CAP : (i + 1) * CAP]

    def dispatch(f, j, i):
        cols = columns(j)

        def block(ref, b):
            return ref.at[f, pl.ds(b * CAP, CAP), cols]

        src, dst, mask = (
            lambda: (rest.at[f, :, cols], rest_p.at[f, :, cols], PAIR),
            lambda: (block(s_d, 0), block(xrows, 6), DIAG),
            lambda: (block(s_y, 0), block(xrows, 4), FAR),
            lambda: (block(s_x, 0), block(xrows, 2), CROSS),
            lambda: (block(s_y, 1), block(xrows, 5), FAR),
            lambda: (block(s_x, 1), block(xrows, 3), CROSS),
            lambda: (block(xrows, 6), block(xrows, 7), PAIR),
        )[i]()
        return remote(src, dst, dis_s.at[f, j, i], dis_r.at[f, j, i], mask)

    def send_own(f, j):
        restore(f, j)
        dispatch(f, j, 0).start()
        pick(f, j, meta, rest, ((xrows, 0), (s_x, 0), (s_y, 0), (s_d, 0)))
        for i in (1, 2, 3):
            dispatch(f, j, i).start()

    def send_partner(f, j):
        dispatch(f, j, 0).wait_recv()
        pick(f, j, meta_p, rest_p, ((xrows, CAP), (s_x, CAP), (s_y, CAP)))
        dispatch(f, j, 4).start()
        dispatch(f, j, 5).start()
        dispatch(f, j, 1).wait_recv()
        dispatch(f, j, 6).start()

    def rows_arrived(f):
        def body(j):
            for i in (2, 3, 4, 5, 6):
                dispatch(f, j, i).wait_recv()

        each(NC, body)

    def hidden(piece):
        turn, ci = divmod(piece, 4)
        f = jnp.where(flip == 1, 1 - turn, turn)
        if ci == 0:
            rows_arrived(f)
        for cp in w_copies(piece):
            cp.wait()
        if piece == 1:
            w_moves[0].wait_recv()
            w_moves[1].wait_recv()
        if piece < 7:
            for cp in w_copies(piece + 1):
                cp.start()

        def step(k, acc):
            rows = pl.ds(pl.multiple_of(k * KC, KC), KC)
            x = xrows[f, :, rows]
            g = jnp.dot(x, wbuf[piece % 2, 0, rows, :], preferred_element_type=F32)
            u = jnp.dot(x, wbuf[piece % 2, 1, rows, :], preferred_element_type=F32)
            return acc[0] + g, acc[1] + u

        zero = jnp.zeros((8 * CAP, HC), F32)
        g, u = lax.fori_loop(0, D // KC, step, (zero, zero))
        hid[f, :, ci * HC : (ci + 1) * HC] = (g / (1.0 + jnp.exp(-g)) * u).astype(BF)

    def combine(f, j, i):
        src, dst, mask = (
            lambda: (g_p.at[f, j, pl.ds(0, CAP)], r_p.at[f, j, pl.ds(0, CAP)], PAIR),
            lambda: (g_x.at[f, j], r_x.at[f, j], CROSS),
            lambda: (g_y.at[f, j], r_y.at[f, j], FAR),
            lambda: (g_t.at[f, j], r_t.at[f, j], PAIR),
            lambda: (g_d.at[f, j], r_d.at[f, j], DIAG),
            lambda: (g_p.at[f, j], r_p.at[f, j], PAIR),
            lambda: (g_y.at[f, j, pl.ds(0, CAP)], r_y.at[f, j, pl.ds(0, CAP)], FAR),
        )[i]()
        return remote(src, dst, com_s.at[f, j, i], com_r.at[f, j, i], mask)

    def handoff(f, j):
        section = jnp.where(f == 0, up, down)
        return remote(fin.at[f, j], out.at[f, :, columns(j)], com_s.at[f, j, 7], com_r.at[f, j, 7], 0, section)

    def gated(f, kind, cols, parts):
        z = jnp.concatenate(parts, axis=0)
        high = jnp.dot(gates[f, kind, 0, :, cols], z, preferred_element_type=F32)
        return high + jnp.dot(gates[f, kind, 1, :, cols], z, preferred_element_type=F32)

    def first(m, f, j):
        for cp in d_copies(m):
            cp.wait()

        @pl.when(m < STEPS - 1)
        def _():
            for cp in d_copies(m + 1):
                cp.start()

        q = jnp.dot(hid[f], dbuf[lax.rem(m, 2)], preferred_element_type=F32).astype(BF)
        g_p[f, j, :CAP] = q[7 * CAP :]
        g_p[f, j, CAP:] = q[5 * CAP : 6 * CAP]
        g_x[f, j] = q[2 * CAP : 4 * CAP]
        keep[f, j] = q[6 * CAP : 7 * CAP]
        g_y[f, j] = q[4 * CAP : 6 * CAP]
        combine(f, j, 1).start()

        @pl.when(summed(f))
        def _():
            combine(f, j, 5).start()

        @pl.when(jnp.logical_not(summed(f)))
        def _():
            combine(f, j, 0).start()
            combine(f, j, 2).start()

        loc[f, j] = q[: 2 * CAP]

    def add(a, b):
        return (a.astype(F32) + b.astype(F32)).astype(BF)

    def second(f, j):
        @pl.when(summed(f))
        def _():
            combine(f, j, 5).wait_recv()
            g_d[f, j] = add(keep[f, j], r_p[f, j, :CAP])
            combine(f, j, 4).start()
            g_y[f, j, :CAP] = add(g_y[f, j, :CAP], r_p[f, j, CAP:])
            combine(f, j, 6).start()
            combine(f, j, 1).wait_recv()
            parts = [loc[f, j, CAP:], r_x[f, j, CAP:]]
            g_t[f, j] = gated(f, 0, slice(0, 2 * CAP), parts).astype(BF)

        @pl.when(jnp.logical_not(summed(f)))
        def _():
            combine(f, j, 0).wait_recv()
            g_d[f, j] = add(keep[f, j], r_p[f, j, :CAP])
            combine(f, j, 4).start()
            combine(f, j, 1).wait_recv()
            combine(f, j, 2).wait_recv()
            parts = [loc[f, j, CAP:], r_x[f, j, CAP:], r_y[f, j, CAP:]]
            g_t[f, j] = gated(f, 0, slice(0, 3 * CAP), parts).astype(BF)

        combine(f, j, 3).start()

    def third(f, j):
        @pl.when(summed(f))
        def _():
            combine(f, j, 6).wait_recv()

        combine(f, j, 4).wait_recv()
        combine(f, j, 3).wait_recv()
        parts = [loc[f, j, :CAP], r_x[f, j, :CAP], r_y[f, j, :CAP], r_d[f, j]]
        total = gated(f, 1, slice(0, 4 * CAP), parts)
        total = total + r_t[f, j].astype(F32) + tokv[f, :, columns(j)].astype(F32)
        fin[f, j] = total.astype(BF)
        handoff(f, j).start()

    def at(step, lag, body):
        n = step - lag

        @pl.when((n >= 0) & (n < STEPS))
        def _():
            turn = n // NC
            body(jnp.where(flip == 1, 1 - turn, turn), n - turn * NC)

    meta[...] = jnp.zeros_like(meta)
    for f in range(2):
        meta[f, 0:2, :TOK] = (ids[f] * (CAP + 1) + slots[f]).astype(F32)
        meta[f, 2:4, :TOK] = gate_in[f]
    meta_move.start()
    for f in range(2):
        tok_copy(f).wait()
    send_own(flip, 0)
    for move in w_moves:
        move.start()
    meta_move.wait_recv()

    def dispatch_step(n):
        @pl.when(n > 0)
        def _():
            at(n, 0, send_own)

        at(n, LAG, send_partner)
        for ci in range(4):

            @pl.when(n == NC + LAG + 1 + ci)
            def _():
                hidden(ci)

    each(STEPS + LAG, dispatch_step)

    w_moves[2].wait_recv()
    for cp in d_copies(0):
        cp.start()
    for f in range(2):
        for kind, table in enumerate((meta_p, meta)):
            gates[f, kind, 0], gates[f, kind, 1] = gating(table, f)

    def combine_step(m):
        at(m, 0, lambda f, j: first(m, f, j))
        for ci in range(4):

            @pl.when(m == 1 + ci)
            def _():
                hidden(4 + ci)

        at(m, LAG, second)
        at(m, 2 * LAG, third)

    each(STEPS + 2 * LAG, combine_step)

    for move in w_moves + [meta_move]:
        move.wait_send()

    def drain(n):
        f = n // NC
        j = n - f * NC
        for i in range(7):
            dispatch(f, j, i).wait_send()
        for i in (1, 3, 4):
            combine(f, j, i).wait_send()

        @pl.when(summed(f))
        def _():
            combine(f, j, 5).wait_send()
            combine(f, j, 6).wait_send()

        @pl.when(jnp.logical_not(summed(f)))
        def _():
            combine(f, j, 0).wait_send()
            combine(f, j, 2).wait_send()

        handoff(f, j).wait()

    each(STEPS, drain)


def local(tokens, route_ids, slot_index, gate_values, w_gate, w_up, w_down):
    routing = [jnp.swapaxes(x[:, 0], 1, 2) for x in (route_ids, slot_index, gate_values)]
    hbm = pl.BlockSpec(memory_space=pltpu.HBM)
    vmem = pl.BlockSpec(memory_space=pltpu.VMEM)
    dma = pltpu.SemaphoreType.DMA

    def buf(*shape):
        return pltpu.VMEM(shape, BF)

    table = pltpu.VMEM((2, 8, 2 * TOK), F32)
    half = buf(2, NC, CAP, CW)
    whole = buf(2, NC, TOK, CW)
    shapes = ((2, TOK, D), (D, H), (D, H), (H, D))
    out = pl.pallas_call(
        kernel,
        out_shape=[jax.ShapeDtypeStruct(shape, BF) for shape in shapes],
        in_specs=[hbm, vmem, vmem, vmem, hbm, hbm, hbm],
        out_specs=[hbm] * 4,
        scratch_shapes=[
            buf(2, TOK, D), buf(2, TOK, D), buf(2, TOK, D), table, table, buf(2, 2, 2, TOK, 4 * CAP),
            buf(2, 8 * CAP, D), buf(2, 2 * CAP, D), buf(2, 2 * CAP, D), buf(2, CAP, D),
            buf(2, 2, D, HC), buf(2, 2 * H, CW), buf(2, 8 * CAP, 2 * H),
            whole, whole, whole, whole, half, half, whole,
            whole, whole, whole, half, whole, whole,
            dma((2,)), dma((2, 2)), dma((2, 2)), dma((3,)), dma((3,)), dma, dma,
            dma((2, NC, 7)), dma((2, NC, 7)), dma((2, NC, 8)), dma((2, NC, 8)),
        ],
        compiler_params=pltpu.CompilerParams(
            collective_id=0, has_side_effects=True, vmem_limit_bytes=63 * 2**20
        ),
        name="relay_layer",
    )(tokens[:, 0], *routing, w_gate[0, 0], w_up[0, 0], w_down[0, 0])
    return out[0][:, None]


def solution(mesh):
    spread = P(None, "section", "expert", None)
    split = P("section", "expert", None, None)
    return jax.shard_map(
        local,
        mesh=mesh,
        in_specs=(spread,) * 4 + (split,) * 3,
        out_specs=spread,
        check_vma=False,
    )
```

```python
import jax
import jax.numpy as jnp
from jax import lax
from jax.experimental import pallas as pl
from jax.experimental.pallas import tpu as pltpu
from jax.sharding import PartitionSpec as P

D = 7168
TILE = 128
TOK = 64
CAP = 32
H = 512
CW = 1024
NC = D // CW
STEPS = 2 * NC
LAG = 4
SECOND = 4
THIRD = 8
LATE = 6
ROW = 4
MESH = pl.DeviceIdType.MESH

CORE = 1
PAIR = 2
CROSS = 6
FAR = 8
DIAG = 14

BF = jnp.bfloat16
F32 = jnp.float32


def coarse(mag):
    lifted = mag * (2.0**20 + 1.0)
    return lifted - (lifted - mag)


def snap(values):
    mag = jnp.abs(values)
    near = coarse(mag)
    mirror = 2.0 * mag - near
    other = coarse(mirror)
    snapped = jnp.where(other == mirror, jnp.maximum(near, other), near)
    fine = jnp.floor(mag * 512.0 + 0.5) * (1.0 / 512.0)
    snapped = jnp.minimum(jnp.where(mag < 2.0**-6, fine, snapped), 448.0)
    return jnp.where(values < 0, -snapped, snapped)


def kernel(
    tok_hbm, ids, slots, gate_in, wg, wu, wd, out, wg2, wu2, wd2,
    tokv, rest, rest_p, meta, meta_p, gates,
    xrows, s_x, s_y, s_d,
    wbuf, dbuf, acc, hid,
    loc, g_x, g_y, g_p, keep, g_d, g_t,
    r_x, r_y, r_p, r_d, r_t, fin,
    tok_sem, w_sem, d_sem, wx_s, wx_r, dx_s, dx_r, meta_s, meta_r,
    dis_s, dis_r, com_s, com_r,
):
    me = lax.axis_index("expert")
    sec = lax.axis_index("section")
    n_sec = lax.axis_size("section")
    up = lax.rem(sec + 1, n_sec)
    down = lax.rem(sec + n_sec - 1, n_sec)
    mine = (me // 8) * 2 + (me // 4) % 2

    flip = (lax.rem(sec, ROW) == 0).astype(jnp.int32)
    ends = (flip == 1) | (lax.rem(sec, ROW) == ROW - 1)

    def summed(f):
        return ends & (f == 1 - flip)

    def remote(src, dst, ss, rs, mask, section=sec):
        return pltpu.make_async_remote_copy(
            src_ref=src, dst_ref=dst, send_sem=ss, recv_sem=rs,
            device_id=(section, me ^ mask), device_id_type=MESH,
        )

    def columns(j):
        return pl.ds(pl.multiple_of(j * CW, CW), CW)

    def each(count, body):
        def step(j, carry):
            body(j)
            return carry

        lax.fori_loop(0, count, step, 0)

    def tok_copy(f):
        return pltpu.make_async_copy(tok_hbm.at[f], tokv.at[f], tok_sem.at[f])

    def w_copies(k):
        slot = lax.rem(k, 2)
        rows = columns(lax.rem(k, NC))
        return [
            pltpu.make_async_copy(src.at[rows], wbuf.at[slot, i], w_sem.at[slot, i])
            for i, src in enumerate((wg, wu, wg2, wu2))
        ]

    def d_copies(m):
        slot = lax.rem(m, 2)
        cols = columns(lax.rem(m, NC))
        return (
            pltpu.make_async_copy(wd.at[:, cols], dbuf.at[slot, pl.ds(0, H)], d_sem.at[slot, 0]),
            pltpu.make_async_copy(wd2.at[:, cols], dbuf.at[slot, pl.ds(H, H)], d_sem.at[slot, 1]),
        )

    for f in range(2):
        tok_copy(f).start()

    barrier = pltpu.get_barrier_semaphore()
    peers = [(sec, mask) for mask in (CORE, PAIR, CROSS, FAR, DIAG)]
    peers += [(up, 0), (down, 0)]
    for section, mask in peers:
        pl.semaphore_signal(barrier, inc=1, device_id=(section, me ^ mask), device_id_type=MESH)
    pl.semaphore_wait(barrier, len(peers))

    def w_move(i, j):
        src, dst = ((wg, wg2), (wu, wu2))[i]
        rows = columns(j)
        return remote(src.at[rows], dst.at[rows], wx_s.at[j, i], wx_r.at[j, i], CORE)

    d_move = remote(wd, wd2, dx_s, dx_r, CORE)
    meta_move = remote(meta, meta_p, meta_s, meta_r, PAIR)

    def restore(f, j):
        for k in range(CW // TILE):
            cols = pl.ds(pl.multiple_of(j * CW, CW) + k * TILE, TILE)
            t = tokv[f, :, cols].astype(F32)
            scale = (jnp.max(jnp.abs(t), axis=-1, keepdims=True) + 1e-6) / 448.0
            rest[f, :, cols] = (snap(t * (1.0 / scale)) * scale).astype(BF)

    def selection(table, f, rows):
        row = lax.broadcasted_iota(jnp.int32, (rows, TOK), 0)
        code = ((mine ^ (row // CAP)) * (CAP + 1) + row % CAP).astype(F32)
        hit = (table[f, 0:1, :TOK] == code) | (table[f, 1:2, :TOK] == code)
        return jnp.where(hit, 1.0, 0.0).astype(BF)

    def gating(table, f):
        row = lax.broadcasted_iota(jnp.int32, (4 * CAP, 2 * TOK), 0)
        code = ((mine ^ (row // CAP)) * (CAP + 1) + row % CAP).astype(F32)
        weight = jnp.where(table[f, 0:1] == code, table[f, 2:3], 0.0)
        weight = weight + jnp.where(table[f, 1:2] == code, table[f, 3:4], 0.0)
        weight = weight.T[:TOK]
        high = weight.astype(BF)
        return high, (weight - high.astype(F32)).astype(BF)

    def pick(f, j, table, source, targets):
        sel = selection(table, f, len(targets) * CAP)
        cols = columns(j)
        got = jnp.dot(sel, source[f, :, cols], preferred_element_type=F32).astype(BF)
        for i, (ref, row) in enumerate(targets):
            ref[f, row : row + CAP, cols] = got[i * CAP : (i + 1) * CAP]

    def dispatch(f, j, i):
        cols = columns(j)

        def block(ref, b):
            return ref.at[f, pl.ds(b * CAP, CAP), cols]

        src, dst, mask = (
            lambda: (rest.at[f, :, cols], rest_p.at[f, :, cols], PAIR),
            lambda: (block(s_d, 0), block(xrows, 6), DIAG),
            lambda: (block(s_y, 0), block(xrows, 4), FAR),
            lambda: (block(s_x, 0), block(xrows, 2), CROSS),
            lambda: (block(s_y, 1), block(xrows, 5), FAR),
            lambda: (block(s_x, 1), block(xrows, 3), CROSS),
            lambda: (block(xrows, 6), block(xrows, 7), PAIR),
        )[i]()
        return remote(src, dst, dis_s.at[f, j, i], dis_r.at[f, j, i], mask)

    def send_own(f, j):
        restore(f, j)
        dispatch(f, j, 0).start()
        pick(f, j, meta, rest, ((xrows, 0), (s_x, 0), (s_y, 0), (s_d, 0)))
        for i in (1, 2, 3):
            dispatch(f, j, i).start()

    def send_partner(f, j):
        dispatch(f, j, 0).wait_recv()
        pick(f, j, meta_p, rest_p, ((xrows, CAP), (s_x, CAP), (s_y, CAP)))
        dispatch(f, j, 4).start()
        dispatch(f, j, 5).start()
        dispatch(f, j, 1).wait_recv()
        dispatch(f, j, 6).start()

    def load_weights(k):
        @pl.when(k < NC)
        def _():
            w_move(0, k).wait_recv()
            w_move(1, k).wait_recv()

        for cp in w_copies(k):
            cp.start()

    def hidden(k, f, j):
        for i in (2, 3, 4, 5, 6):
            dispatch(f, j, i).wait_recv()
        for cp in w_copies(k):
            cp.wait()

        @pl.when(k < STEPS - 1)
        def _():
            load_weights(k + 1)

        @pl.when(j == 0)
        def _():
            acc[...] = jnp.zeros_like(acc)

        x = xrows[f, :, columns(j)]
        for i in range(4):
            acc[i] += jnp.dot(x, wbuf[lax.rem(k, 2), i], preferred_element_type=F32)

        @pl.when(j == NC - 1)
        def _():
            for i in range(2):
                g = acc[2 * i]
                hid[f, :, i * H : (i + 1) * H] = (g / (1.0 + jnp.exp(-g)) * acc[2 * i + 1]).astype(BF)

    def combine(f, j, i):
        src, dst, mask = (
            lambda: (g_p.at[f, j, pl.ds(0, CAP)], r_p.at[f, j, pl.ds(0, CAP)], PAIR),
            lambda: (g_x.at[f, j], r_x.at[f, j], CROSS),
            lambda: (g_y.at[f, j], r_y.at[f, j], FAR),
            lambda: (g_t.at[f, j], r_t.at[f, j], PAIR),
            lambda: (g_d.at[f, j], r_d.at[f, j], DIAG),
            lambda: (g_p.at[f, j], r_p.at[f, j], PAIR),
            lambda: (g_y.at[f, j, pl.ds(0, CAP)], r_y.at[f, j, pl.ds(0, CAP)], FAR),
        )[i]()
        return remote(src, dst, com_s.at[f, j, i], com_r.at[f, j, i], mask)

    def handoff(f, j):
        section = jnp.where(f == 0, up, down)
        return remote(fin.at[f, j], out.at[f, :, columns(j)], com_s.at[f, j, 7], com_r.at[f, j, 7], 0, section)

    def gated(f, kind, cols, parts):
        z = jnp.concatenate(parts, axis=0)
        high = jnp.dot(gates[f, kind, 0, :, cols], z, preferred_element_type=F32)
        return high + jnp.dot(gates[f, kind, 1, :, cols], z, preferred_element_type=F32)

    def first(m, f, j):
        for cp in d_copies(m):
            cp.wait()

        @pl.when(m < STEPS - 1)
        def _():
            for cp in d_copies(m + 1):
                cp.start()

        q = jnp.dot(hid[f], dbuf[lax.rem(m, 2)], preferred_element_type=F32).astype(BF)
        g_p[f, j, :CAP] = q[7 * CAP :]
        g_p[f, j, CAP:] = q[5 * CAP : 6 * CAP]
        g_x[f, j] = q[2 * CAP : 4 * CAP]
        keep[f, j] = q[6 * CAP : 7 * CAP]
        g_y[f, j] = q[4 * CAP : 6 * CAP]
        combine(f, j, 1).start()

        @pl.when(summed(f))
        def _():
            combine(f, j, 5).start()

        @pl.when(jnp.logical_not(summed(f)))
        def _():
            combine(f, j, 0).start()
            combine(f, j, 2).start()

        loc[f, j] = q[: 2 * CAP]

    def add(a, b):
        return (a.astype(F32) + b.astype(F32)).astype(BF)

    def second(f, j):
        @pl.when(summed(f))
        def _():
            combine(f, j, 5).wait_recv()
            g_d[f, j] = add(keep[f, j], r_p[f, j, :CAP])
            combine(f, j, 4).start()
            g_y[f, j, :CAP] = add(g_y[f, j, :CAP], r_p[f, j, CAP:])
            combine(f, j, 6).start()
            combine(f, j, 1).wait_recv()
            parts = [loc[f, j, CAP:], r_x[f, j, CAP:]]
            g_t[f, j] = gated(f, 0, slice(0, 2 * CAP), parts).astype(BF)

        @pl.when(jnp.logical_not(summed(f)))
        def _():
            combine(f, j, 0).wait_recv()
            g_d[f, j] = add(keep[f, j], r_p[f, j, :CAP])
            combine(f, j, 4).start()
            combine(f, j, 1).wait_recv()
            combine(f, j, 2).wait_recv()
            parts = [loc[f, j, CAP:], r_x[f, j, CAP:], r_y[f, j, CAP:]]
            g_t[f, j] = gated(f, 0, slice(0, 3 * CAP), parts).astype(BF)

        combine(f, j, 3).start()

    def third(f, j):
        @pl.when(summed(f))
        def _():
            combine(f, j, 6).wait_recv()

        combine(f, j, 4).wait_recv()
        combine(f, j, 3).wait_recv()
        parts = [loc[f, j, :CAP], r_x[f, j, :CAP], r_y[f, j, :CAP], r_d[f, j]]
        total = gated(f, 1, slice(0, 4 * CAP), parts)
        total = total + r_t[f, j].astype(F32) + tokv[f, :, columns(j)].astype(F32)
        fin[f, j] = total.astype(BF)
        handoff(f, j).start()

    def at(step, lag, body):
        n = step - lag

        @pl.when((n >= 0) & (n < STEPS))
        def _():
            turn = n // NC
            body(jnp.where(flip == 1, 1 - turn, turn), n - turn * NC)

    meta[...] = jnp.zeros_like(meta)
    for f in range(2):
        meta[f, 0:2, :TOK] = (ids[f] * (CAP + 1) + slots[f]).astype(F32)
        meta[f, 2:4, :TOK] = gate_in[f]
    meta_move.start()
    for f in range(2):
        tok_copy(f).wait()
    send_own(flip, 0)
    for j in range(NC):
        w_move(0, j).start()
        w_move(1, j).start()
    d_move.start()
    meta_move.wait_recv()
    for f in range(2):
        for kind, table in enumerate((meta_p, meta)):
            gates[f, kind, 0], gates[f, kind, 1] = gating(table, f)

    def step(n):
        @pl.when(n > 0)
        def _():
            at(n, 0, send_own)

        at(n, LAG, send_partner)

        @pl.when(n == LATE - 1)
        def _():
            load_weights(0)

        @pl.when(n == STEPS - 1)
        def _():
            d_move.wait_recv()
            for cp in d_copies(0):
                cp.start()

        at(n, STEPS, lambda f, j: first(n - STEPS, f, j))
        at(n, STEPS + SECOND, second)
        at(n, STEPS + THIRD, third)
        at(n, LATE, lambda f, j: hidden(n - LATE, f, j))

    each(2 * STEPS + THIRD, step)

    meta_move.wait_send()
    d_move.wait_send()

    def drain_weights(j):
        w_move(0, j).wait_send()
        w_move(1, j).wait_send()

    each(NC, drain_weights)

    def drain(n):
        f = n // NC
        j = n - f * NC
        for i in range(7):
            dispatch(f, j, i).wait_send()
        for i in (1, 3, 4):
            combine(f, j, i).wait_send()

        @pl.when(summed(f))
        def _():
            combine(f, j, 5).wait_send()
            combine(f, j, 6).wait_send()

        @pl.when(jnp.logical_not(summed(f)))
        def _():
            combine(f, j, 0).wait_send()
            combine(f, j, 2).wait_send()

        handoff(f, j).wait()

    each(STEPS, drain)


def local(tokens, route_ids, slot_index, gate_values, w_gate, w_up, w_down):
    routing = [jnp.swapaxes(x[:, 0], 1, 2) for x in (route_ids, slot_index, gate_values)]
    hbm = pl.BlockSpec(memory_space=pltpu.HBM)
    vmem = pl.BlockSpec(memory_space=pltpu.VMEM)
    dma = pltpu.SemaphoreType.DMA

    def buf(*shape):
        return pltpu.VMEM(shape, BF)

    table = pltpu.VMEM((2, 8, 2 * TOK), F32)
    half = buf(2, NC, CAP, CW)
    whole = buf(2, NC, TOK, CW)
    shapes = ((2, TOK, D), (D, H), (D, H), (H, D))
    out = pl.pallas_call(
        kernel,
        out_shape=[jax.ShapeDtypeStruct(shape, BF) for shape in shapes],
        in_specs=[hbm, vmem, vmem, vmem, hbm, hbm, hbm],
        out_specs=[hbm] * 4,
        scratch_shapes=[
            buf(2, TOK, D), buf(2, TOK, D), buf(2, TOK, D), table, table, buf(2, 2, 2, TOK, 4 * CAP),
            buf(2, 8 * CAP, D), buf(2, 2 * CAP, D), buf(2, 2 * CAP, D), buf(2, CAP, D),
            buf(2, 4, CW, H), buf(2, 2 * H, CW), pltpu.VMEM((4, 8 * CAP, H), F32), buf(2, 8 * CAP, 2 * H),
            whole, whole, whole, whole, half, half, whole,
            whole, whole, whole, half, whole, whole,
            dma((2,)), dma((2, 4)), dma((2, 2)), dma((NC, 2)), dma((NC, 2)), dma, dma, dma, dma,
            dma((2, NC, 7)), dma((2, NC, 7)), dma((2, NC, 8)), dma((2, NC, 8)),
        ],
        compiler_params=pltpu.CompilerParams(
            collective_id=0, has_side_effects=True, vmem_limit_bytes=63 * 2**20
        ),
        name="relay_layer",
    )(tokens[:, 0], *routing, w_gate[0, 0], w_up[0, 0], w_down[0, 0])
    return out[0][:, None]


def solution(mesh):
    spread = P(None, "section", "expert", None)
    split = P("section", "expert", None, None)
    return jax.shard_map(
        local,
        mesh=mesh,
        in_specs=(spread,) * 4 + (split,) * 3,
        out_specs=spread,
        check_vma=False,
    )
```

```python
import jax
import jax.numpy as jnp
from jax import lax
from jax.experimental import pallas as pl
from jax.experimental.pallas import tpu as pltpu
from jax.sharding import PartitionSpec as P

D = 7168
TILE = 128
TOK = 64
CAP = 32
H = 512
CW = 1024
NC = D // CW
STEPS = 2 * NC
LAG = 4
SECOND = 4
THIRD = 8
RELAY = 10
SUMMED = 5
LATE = 6
ROW = 4
MESH = pl.DeviceIdType.MESH

CORE = 1
PAIR = 2
CROSS = 6
FAR = 8
DIAG = 14

BF = jnp.bfloat16
F32 = jnp.float32


def coarse(mag):
    lifted = mag * (2.0**20 + 1.0)
    return lifted - (lifted - mag)


def snap(values):
    mag = jnp.abs(values)
    near = coarse(mag)
    mirror = 2.0 * mag - near
    other = coarse(mirror)
    snapped = jnp.where(other == mirror, jnp.maximum(near, other), near)
    fine = jnp.floor(mag * 512.0 + 0.5) * (1.0 / 512.0)
    snapped = jnp.minimum(jnp.where(mag < 2.0**-6, fine, snapped), 448.0)
    return jnp.where(values < 0, -snapped, snapped)


def kernel(
    tok_hbm, ids, slots, gate_in, wg, wu, wd, out, wg2, wu2, wd2,
    tokv, rest, rest_p, meta, meta_p, gates,
    xrows, s_x, s_y, s_d,
    wbuf, dbuf, acc, hid,
    loc, g_x, g_y, g_p, keep, g_d, g_t,
    r_x, r_y, r_p, r_d, r_t, fin, half_way,
    tok_sem, w_sem, d_sem, wx_s, wx_r, dx_s, dx_r, meta_s, meta_r,
    dis_s, dis_r, com_s, com_r, way_s, way_r, last_r,
):
    me = lax.axis_index("expert")
    sec = lax.axis_index("section")
    n_sec = lax.axis_size("section")
    up = lax.rem(sec + 1, n_sec)
    down = lax.rem(sec + n_sec - 1, n_sec)
    mine = (me // 8) * 2 + (me // 4) % 2

    flip = (lax.rem(sec, ROW) == 0).astype(jnp.int32)
    ends = (flip == 1) | (lax.rem(sec, ROW) == ROW - 1)
    to_relay = sec ^ (ROW + 1)
    from_relay = sec ^ 2

    def wraps(f):
        return ends & (f == flip)

    def arrives(f):
        return ends & (f == 1 - flip)

    def summed(f, j):
        return (f == 1 - flip) & (j < SUMMED)

    def remote(src, dst, ss, rs, mask, section=sec):
        return pltpu.make_async_remote_copy(
            src_ref=src, dst_ref=dst, send_sem=ss, recv_sem=rs,
            device_id=(section, me ^ mask), device_id_type=MESH,
        )

    def columns(j):
        return pl.ds(pl.multiple_of(j * CW, CW), CW)

    def each(count, body):
        def step(j, carry):
            body(j)
            return carry

        lax.fori_loop(0, count, step, 0)

    def tok_copy(f):
        return pltpu.make_async_copy(tok_hbm.at[f], tokv.at[f], tok_sem.at[f])

    def w_copies(k):
        slot = lax.rem(k, 2)
        rows = columns(lax.rem(k, NC))
        return [
            pltpu.make_async_copy(src.at[rows], wbuf.at[slot, i], w_sem.at[slot, i])
            for i, src in enumerate((wg, wu, wg2, wu2))
        ]

    def d_copies(m):
        slot = lax.rem(m, 2)
        cols = columns(lax.rem(m, NC))
        return (
            pltpu.make_async_copy(wd.at[:, cols], dbuf.at[slot, pl.ds(0, H)], d_sem.at[slot, 0]),
            pltpu.make_async_copy(wd2.at[:, cols], dbuf.at[slot, pl.ds(H, H)], d_sem.at[slot, 1]),
        )

    for f in range(2):
        tok_copy(f).start()

    barrier = pltpu.get_barrier_semaphore()
    peers = [(sec, mask) for mask in (CORE, PAIR, CROSS, FAR, DIAG)]
    peers += [(up, 0), (down, 0), (to_relay, 0), (from_relay, 0)]
    for section, mask in peers:
        pl.semaphore_signal(barrier, inc=1, device_id=(section, me ^ mask), device_id_type=MESH)
    pl.semaphore_wait(barrier, len(peers))

    def w_move(i, j):
        src, dst = ((wg, wg2), (wu, wu2))[i]
        rows = columns(j)
        return remote(src.at[rows], dst.at[rows], wx_s.at[j, i], wx_r.at[j, i], CORE)

    d_move = remote(wd, wd2, dx_s, dx_r, CORE)
    meta_move = remote(meta, meta_p, meta_s, meta_r, PAIR)

    def restore(f, j):
        for k in range(CW // TILE):
            cols = pl.ds(pl.multiple_of(j * CW, CW) + k * TILE, TILE)
            t = tokv[f, :, cols].astype(F32)
            scale = (jnp.max(jnp.abs(t), axis=-1, keepdims=True) + 1e-6) / 448.0
            rest[f, :, cols] = (snap(t * (1.0 / scale)) * scale).astype(BF)

    def selection(table, f, rows):
        row = lax.broadcasted_iota(jnp.int32, (rows, TOK), 0)
        code = ((mine ^ (row // CAP)) * (CAP + 1) + row % CAP).astype(F32)
        hit = (table[f, 0:1, :TOK] == code) | (table[f, 1:2, :TOK] == code)
        return jnp.where(hit, 1.0, 0.0).astype(BF)

    def gating(table, f):
        row = lax.broadcasted_iota(jnp.int32, (4 * CAP, 2 * TOK), 0)
        code = ((mine ^ (row // CAP)) * (CAP + 1) + row % CAP).astype(F32)
        weight = jnp.where(table[f, 0:1] == code, table[f, 2:3], 0.0)
        weight = weight + jnp.where(table[f, 1:2] == code, table[f, 3:4], 0.0)
        weight = weight.T[:TOK]
        high = weight.astype(BF)
        return high, (weight - high.astype(F32)).astype(BF)

    def pick(f, j, table, source, targets):
        sel = selection(table, f, len(targets) * CAP)
        cols = columns(j)
        got = jnp.dot(sel, source[f, :, cols], preferred_element_type=F32).astype(BF)
        for i, (ref, row) in enumerate(targets):
            ref[f, row : row + CAP, cols] = got[i * CAP : (i + 1) * CAP]

    def dispatch(f, j, i):
        cols = columns(j)

        def block(ref, b):
            return ref.at[f, pl.ds(b * CAP, CAP), cols]

        src, dst, mask = (
            lambda: (rest.at[f, :, cols], rest_p.at[f, :, cols], PAIR),
            lambda: (block(s_d, 0), block(xrows, 6), DIAG),
            lambda: (block(s_y, 0), block(xrows, 4), FAR),
            lambda: (block(s_x, 0), block(xrows, 2), CROSS),
            lambda: (block(s_y, 1), block(xrows, 5), FAR),
            lambda: (block(s_x, 1), block(xrows, 3), CROSS),
            lambda: (block(xrows, 6), block(xrows, 7), PAIR),
        )[i]()
        return remote(src, dst, dis_s.at[f, j, i], dis_r.at[f, j, i], mask)

    def send_own(f, j):
        restore(f, j)
        dispatch(f, j, 0).start()
        pick(f, j, meta, rest, ((xrows, 0), (s_x, 0), (s_y, 0), (s_d, 0)))
        for i in (1, 2, 3):
            dispatch(f, j, i).start()

    def send_partner(f, j):
        dispatch(f, j, 0).wait_recv()
        pick(f, j, meta_p, rest_p, ((xrows, CAP), (s_x, CAP), (s_y, CAP)))
        dispatch(f, j, 4).start()
        dispatch(f, j, 5).start()
        dispatch(f, j, 1).wait_recv()
        dispatch(f, j, 6).start()

    def load_weights(k):
        @pl.when(k < NC)
        def _():
            w_move(0, k).wait_recv()
            w_move(1, k).wait_recv()

        for cp in w_copies(k):
            cp.start()

    def hidden(k, f, j):
        for i in (2, 3, 4, 5, 6):
            dispatch(f, j, i).wait_recv()
        for cp in w_copies(k):
            cp.wait()

        @pl.when(k < STEPS - 1)
        def _():
            load_weights(k + 1)

        @pl.when(j == 0)
        def _():
            acc[...] = jnp.zeros_like(acc)

        x = xrows[f, :, columns(j)]
        for i in range(4):
            acc[i] += jnp.dot(x, wbuf[lax.rem(k, 2), i], preferred_element_type=F32)

        @pl.when(j == NC - 1)
        def _():
            for i in range(2):
                g = acc[2 * i]
                hid[f, :, i * H : (i + 1) * H] = (g / (1.0 + jnp.exp(-g)) * acc[2 * i + 1]).astype(BF)

    def combine(f, j, i):
        src, dst, mask = (
            lambda: (g_p.at[f, j, pl.ds(0, CAP)], r_p.at[f, j, pl.ds(0, CAP)], PAIR),
            lambda: (g_x.at[f, j], r_x.at[f, j], CROSS),
            lambda: (g_y.at[f, j], r_y.at[f, j], FAR),
            lambda: (g_t.at[f, j], r_t.at[f, j], PAIR),
            lambda: (g_d.at[f, j], r_d.at[f, j], DIAG),
            lambda: (g_p.at[f, j], r_p.at[f, j], PAIR),
            lambda: (g_y.at[f, j, pl.ds(0, CAP)], r_y.at[f, j, pl.ds(0, CAP)], FAR),
        )[i]()
        return remote(src, dst, com_s.at[f, j, i], com_r.at[f, j, i], mask)

    def handoff(f, j):
        section = jnp.where(f == 0, up, down)
        return remote(fin.at[f, j], out.at[f, :, columns(j)], com_s.at[f, j, 7], com_r.at[f, j, 7], 0, section)

    def first_half(f, j):
        section = jnp.where(f == 0, up, down)
        rows = pl.ds(0, CAP)
        return remote(fin.at[f, j, rows], out.at[f, rows, columns(j)], com_s.at[f, j, 7], com_r.at[f, j, 7], 0, section)

    def second_half(f, j):
        return remote(fin.at[f, j, pl.ds(CAP, CAP)], half_way.at[j], way_s.at[j], way_r.at[j], 0, to_relay)

    def relayed(f, j):
        return remote(half_way.at[j], out.at[f, pl.ds(CAP, CAP), columns(j)], way_s.at[j], last_r.at[j], 0, from_relay)

    def hand_over(f, j):
        @pl.when(wraps(f))
        def _():
            first_half(f, j).start()
            second_half(f, j).start()

        @pl.when(jnp.logical_not(wraps(f)))
        def _():
            handoff(f, j).start()

    front_between = (lax.rem(sec, ROW) == 1).astype(jnp.int32)

    def relay(j):
        second_half(front_between, j).wait_recv()
        relayed(front_between, j).start()

    def gated(f, kind, cols, parts):
        z = jnp.concatenate(parts, axis=0)
        high = jnp.dot(gates[f, kind, 0, :, cols], z, preferred_element_type=F32)
        return high + jnp.dot(gates[f, kind, 1, :, cols], z, preferred_element_type=F32)

    def first(m, f, j):
        for cp in d_copies(m):
            cp.wait()

        @pl.when(m < STEPS - 1)
        def _():
            for cp in d_copies(m + 1):
                cp.start()

        q = jnp.dot(hid[f], dbuf[lax.rem(m, 2)], preferred_element_type=F32).astype(BF)
        g_p[f, j, :CAP] = q[7 * CAP :]
        g_p[f, j, CAP:] = q[5 * CAP : 6 * CAP]
        g_x[f, j] = q[2 * CAP : 4 * CAP]
        keep[f, j] = q[6 * CAP : 7 * CAP]
        g_y[f, j] = q[4 * CAP : 6 * CAP]
        combine(f, j, 1).start()

        @pl.when(summed(f, j))
        def _():
            combine(f, j, 5).start()

        @pl.when(jnp.logical_not(summed(f, j)))
        def _():
            combine(f, j, 0).start()
            combine(f, j, 2).start()

        loc[f, j] = q[: 2 * CAP]

    def add(a, b):
        return (a.astype(F32) + b.astype(F32)).astype(BF)

    def second(f, j):
        @pl.when(summed(f, j))
        def _():
            combine(f, j, 5).wait_recv()
            g_d[f, j] = add(keep[f, j], r_p[f, j, :CAP])
            combine(f, j, 4).start()
            g_y[f, j, :CAP] = add(g_y[f, j, :CAP], r_p[f, j, CAP:])
            combine(f, j, 6).start()
            combine(f, j, 1).wait_recv()
            parts = [loc[f, j, CAP:], r_x[f, j, CAP:]]
            g_t[f, j] = gated(f, 0, slice(0, 2 * CAP), parts).astype(BF)

        @pl.when(jnp.logical_not(summed(f, j)))
        def _():
            combine(f, j, 0).wait_recv()
            g_d[f, j] = add(keep[f, j], r_p[f, j, :CAP])
            combine(f, j, 4).start()
            combine(f, j, 1).wait_recv()
            combine(f, j, 2).wait_recv()
            parts = [loc[f, j, CAP:], r_x[f, j, CAP:], r_y[f, j, CAP:]]
            g_t[f, j] = gated(f, 0, slice(0, 3 * CAP), parts).astype(BF)

        combine(f, j, 3).start()

    def third(f, j):
        @pl.when(summed(f, j))
        def _():
            combine(f, j, 6).wait_recv()

        combine(f, j, 4).wait_recv()
        combine(f, j, 3).wait_recv()
        parts = [loc[f, j, :CAP], r_x[f, j, :CAP], r_y[f, j, :CAP], r_d[f, j]]
        total = gated(f, 1, slice(0, 4 * CAP), parts)
        total = total + r_t[f, j].astype(F32) + tokv[f, :, columns(j)].astype(F32)
        fin[f, j] = total.astype(BF)
        hand_over(f, j)

    def at(step, lag, body):
        n = step - lag

        @pl.when((n >= 0) & (n < STEPS))
        def _():
            turn = n // NC
            body(jnp.where(flip == 1, 1 - turn, turn), n - turn * NC)

    meta[...] = jnp.zeros_like(meta)
    for f in range(2):
        meta[f, 0:2, :TOK] = (ids[f] * (CAP + 1) + slots[f]).astype(F32)
        meta[f, 2:4, :TOK] = gate_in[f]
    meta_move.start()
    for f in range(2):
        tok_copy(f).wait()
    send_own(flip, 0)
    for j in range(NC):
        w_move(0, j).start()
        w_move(1, j).start()
    d_move.start()
    meta_move.wait_recv()
    for f in range(2):
        for kind, table in enumerate((meta_p, meta)):
            gates[f, kind, 0], gates[f, kind, 1] = gating(table, f)

    def step(n):
        @pl.when(n > 0)
        def _():
            at(n, 0, send_own)

        at(n, LAG, send_partner)

        @pl.when(n == LATE - 1)
        def _():
            load_weights(0)

        @pl.when(n == STEPS - 1)
        def _():
            d_move.wait_recv()
            for cp in d_copies(0):
                cp.start()

        at(n, STEPS, lambda f, j: first(n - STEPS, f, j))
        at(n, STEPS + SECOND, second)
        at(n, STEPS + THIRD, third)
        at(n, LATE, lambda f, j: hidden(n - LATE, f, j))

        @pl.when(jnp.logical_not(ends) & (n >= STEPS + RELAY) & (n < STEPS + RELAY + NC))
        def _():
            relay(n - STEPS - RELAY)


    each(2 * STEPS + THIRD, step)

    meta_move.wait_send()
    d_move.wait_send()

    def drain_weights(j):
        w_move(0, j).wait_send()
        w_move(1, j).wait_send()

    each(NC, drain_weights)

    def drain(n):
        f = n // NC
        j = n - f * NC
        for i in range(7):
            dispatch(f, j, i).wait_send()
        for i in (1, 3, 4):
            combine(f, j, i).wait_send()

        @pl.when(summed(f, j))
        def _():
            combine(f, j, 5).wait_send()
            combine(f, j, 6).wait_send()

        @pl.when(jnp.logical_not(summed(f, j)))
        def _():
            combine(f, j, 0).wait_send()
            combine(f, j, 2).wait_send()

        @pl.when(wraps(f))
        def _():
            first_half(f, j).wait_send()
            second_half(f, j).wait_send()

        @pl.when(jnp.logical_not(wraps(f)))
        def _():
            handoff(f, j).wait_send()

        @pl.when(arrives(f))
        def _():
            first_half(f, j).wait_recv()
            relayed(f, j).wait_recv()

        @pl.when(jnp.logical_not(arrives(f)))
        def _():
            handoff(f, j).wait_recv()


    each(STEPS, drain)

    @pl.when(jnp.logical_not(ends))
    def _():
        each(NC, lambda j: relayed(front_between, j).wait_send())


def local(tokens, route_ids, slot_index, gate_values, w_gate, w_up, w_down):
    routing = [jnp.swapaxes(x[:, 0], 1, 2) for x in (route_ids, slot_index, gate_values)]
    hbm = pl.BlockSpec(memory_space=pltpu.HBM)
    vmem = pl.BlockSpec(memory_space=pltpu.VMEM)
    dma = pltpu.SemaphoreType.DMA

    def buf(*shape):
        return pltpu.VMEM(shape, BF)

    table = pltpu.VMEM((2, 8, 2 * TOK), F32)
    half = buf(2, NC, CAP, CW)
    whole = buf(2, NC, TOK, CW)
    shapes = ((2, TOK, D), (D, H), (D, H), (H, D))
    out = pl.pallas_call(
        kernel,
        out_shape=[jax.ShapeDtypeStruct(shape, BF) for shape in shapes],
        in_specs=[hbm, vmem, vmem, vmem, hbm, hbm, hbm],
        out_specs=[hbm] * 4,
        scratch_shapes=[
            buf(2, TOK, D), buf(2, TOK, D), buf(2, TOK, D), table, table, buf(2, 2, 2, TOK, 4 * CAP),
            buf(2, 8 * CAP, D), buf(2, 2 * CAP, D), buf(2, 2 * CAP, D), buf(2, CAP, D),
            buf(2, 4, CW, H), buf(2, 2 * H, CW), pltpu.VMEM((4, 8 * CAP, H), F32), buf(2, 8 * CAP, 2 * H),
            whole, whole, whole, whole, half, half, whole,
            whole, whole, whole, half, whole, whole, buf(NC, CAP, CW),
            dma((2,)), dma((2, 4)), dma((2, 2)), dma((NC, 2)), dma((NC, 2)), dma, dma, dma, dma,
            dma((2, NC, 7)), dma((2, NC, 7)), dma((2, NC, 8)), dma((2, NC, 8)), dma((NC,)), dma((NC,)), dma((NC,)),
        ],
        compiler_params=pltpu.CompilerParams(
            collective_id=0, has_side_effects=True, vmem_limit_bytes=63 * 2**20
        ),
        name="relay_layer",
    )(tokens[:, 0], *routing, w_gate[0, 0], w_up[0, 0], w_down[0, 0])
    return out[0][:, None]


def solution(mesh):
    spread = P(None, "section", "expert", None)
    split = P("section", "expert", None, None)
    return jax.shard_map(
        local,
        mesh=mesh,
        in_specs=(spread,) * 4 + (split,) * 3,
        out_specs=spread,
        check_vma=False,
    )
```

```python
import jax
import jax.numpy as jnp
from jax import lax
from jax.experimental import pallas as pl
from jax.experimental.pallas import tpu as pltpu
from jax.sharding import PartitionSpec as P

D = 7168
TILE = 128
TOK = 64
CAP = 32
H = 512
CW = 1024
NC = D // CW
STEPS = 2 * NC
LAG = 4
SECOND = 4
THIRD = 7
RELAY = 9
SUMMED = 5
LATE = 6
ROW = 4
MESH = pl.DeviceIdType.MESH

CORE = 1
PAIR = 2
CROSS = 6
FAR = 8
DIAG = 14

BF = jnp.bfloat16
F32 = jnp.float32


def coarse(mag):
    lifted = mag * (2.0**20 + 1.0)
    return lifted - (lifted - mag)


def snap(values):
    mag = jnp.abs(values)
    near = coarse(mag)
    mirror = 2.0 * mag - near
    other = coarse(mirror)
    snapped = jnp.where(other == mirror, jnp.maximum(near, other), near)
    fine = jnp.floor(mag * 512.0 + 0.5) * (1.0 / 512.0)
    snapped = jnp.minimum(jnp.where(mag < 2.0**-6, fine, snapped), 448.0)
    return jnp.where(values < 0, -snapped, snapped)


def kernel(
    tok_hbm, ids, slots, gate_in, wg, wu, wd, out, wg2, wu2, wd2,
    tokv, rest, rest_p, meta, meta_p, gates,
    xrows, s_x, s_y, s_d,
    wbuf, dbuf, acc, hid,
    loc, g_x, g_y, g_p, keep, g_d, g_t,
    r_x, r_y, r_p, r_d, r_t, fin, half_way,
    tok_sem, w_sem, d_sem, wx_s, wx_r, dx_s, dx_r, meta_s, meta_r,
    dis_s, dis_r, com_s, com_r, way_s, way_r, last_r,
):
    me = lax.axis_index("expert")
    sec = lax.axis_index("section")
    n_sec = lax.axis_size("section")
    up = lax.rem(sec + 1, n_sec)
    down = lax.rem(sec + n_sec - 1, n_sec)
    mine = (me // 8) * 2 + (me // 4) % 2

    flip = (lax.rem(sec, ROW) == 0).astype(jnp.int32)
    ends = (flip == 1) | (lax.rem(sec, ROW) == ROW - 1)
    to_relay = sec ^ (ROW + 1)
    from_relay = sec ^ 2

    def wraps(f):
        return ends & (f == flip)

    def arrives(f):
        return ends & (f == 1 - flip)

    def summed(f, j):
        return (f == 1 - flip) & (j < SUMMED)

    def remote(src, dst, ss, rs, mask, section=sec):
        return pltpu.make_async_remote_copy(
            src_ref=src, dst_ref=dst, send_sem=ss, recv_sem=rs,
            device_id=(section, me ^ mask), device_id_type=MESH,
        )

    def columns(j):
        return pl.ds(pl.multiple_of(j * CW, CW), CW)

    def each(count, body):
        def step(j, carry):
            body(j)
            return carry

        lax.fori_loop(0, count, step, 0)

    def tok_copy(f):
        return pltpu.make_async_copy(tok_hbm.at[f], tokv.at[f], tok_sem.at[f])

    def w_copies(k):
        slot = lax.rem(k, 2)
        rows = columns(lax.rem(k, NC))
        return [
            pltpu.make_async_copy(src.at[rows], wbuf.at[slot, i], w_sem.at[slot, i])
            for i, src in enumerate((wg, wu, wg2, wu2))
        ]

    def d_copies(m):
        slot = lax.rem(m, 2)
        cols = columns(lax.rem(m, NC))
        return (
            pltpu.make_async_copy(wd.at[:, cols], dbuf.at[slot, pl.ds(0, H)], d_sem.at[slot, 0]),
            pltpu.make_async_copy(wd2.at[:, cols], dbuf.at[slot, pl.ds(H, H)], d_sem.at[slot, 1]),
        )

    for f in range(2):
        tok_copy(f).start()

    barrier = pltpu.get_barrier_semaphore()
    peers = [(sec, mask) for mask in (CORE, PAIR, CROSS, FAR, DIAG)]
    peers += [(up, 0), (down, 0), (to_relay, 0), (from_relay, 0)]
    for section, mask in peers:
        pl.semaphore_signal(barrier, inc=1, device_id=(section, me ^ mask), device_id_type=MESH)
    pl.semaphore_wait(barrier, len(peers))

    def w_move(i, j):
        src, dst = ((wg, wg2), (wu, wu2))[i]
        rows = columns(j)
        return remote(src.at[rows], dst.at[rows], wx_s.at[j, i], wx_r.at[j, i], CORE)

    d_move = remote(wd, wd2, dx_s, dx_r, CORE)
    meta_move = remote(meta, meta_p, meta_s, meta_r, PAIR)

    def restore(f, j):
        for k in range(CW // TILE):
            cols = pl.ds(pl.multiple_of(j * CW, CW) + k * TILE, TILE)
            t = tokv[f, :, cols].astype(F32)
            scale = (jnp.max(jnp.abs(t), axis=-1, keepdims=True) + 1e-6) / 448.0
            rest[f, :, cols] = (snap(t * (1.0 / scale)) * scale).astype(BF)

    def selection(table, f, rows):
        row = lax.broadcasted_iota(jnp.int32, (rows, TOK), 0)
        code = ((mine ^ (row // CAP)) * (CAP + 1) + row % CAP).astype(F32)
        hit = (table[f, 0:1, :TOK] == code) | (table[f, 1:2, :TOK] == code)
        return jnp.where(hit, 1.0, 0.0).astype(BF)

    def gating(table, f):
        row = lax.broadcasted_iota(jnp.int32, (4 * CAP, 2 * TOK), 0)
        code = ((mine ^ (row // CAP)) * (CAP + 1) + row % CAP).astype(F32)
        weight = jnp.where(table[f, 0:1] == code, table[f, 2:3], 0.0)
        weight = weight + jnp.where(table[f, 1:2] == code, table[f, 3:4], 0.0)
        weight = weight.T[:TOK]
        high = weight.astype(BF)
        return high, (weight - high.astype(F32)).astype(BF)

    def pick(f, j, table, source, targets):
        sel = selection(table, f, len(targets) * CAP)
        cols = columns(j)
        got = jnp.dot(sel, source[f, :, cols], preferred_element_type=F32).astype(BF)
        for i, (ref, row) in enumerate(targets):
            ref[f, row : row + CAP, cols] = got[i * CAP : (i + 1) * CAP]

    def dispatch(f, j, i):
        cols = columns(j)

        def block(ref, b):
            return ref.at[f, pl.ds(b * CAP, CAP), cols]

        src, dst, mask = (
            lambda: (rest.at[f, :, cols], rest_p.at[f, :, cols], PAIR),
            lambda: (block(s_d, 0), block(xrows, 6), DIAG),
            lambda: (block(s_y, 0), block(xrows, 4), FAR),
            lambda: (block(s_x, 0), block(xrows, 2), CROSS),
            lambda: (block(s_y, 1), block(xrows, 5), FAR),
            lambda: (block(s_x, 1), block(xrows, 3), CROSS),
            lambda: (block(xrows, 6), block(xrows, 7), PAIR),
        )[i]()
        return remote(src, dst, dis_s.at[f, j, i], dis_r.at[f, j, i], mask)

    def send_own(f, j):
        restore(f, j)
        dispatch(f, j, 0).start()
        pick(f, j, meta, rest, ((xrows, 0), (s_x, 0), (s_y, 0), (s_d, 0)))
        for i in (1, 2, 3):
            dispatch(f, j, i).start()

    def send_partner(f, j):
        dispatch(f, j, 0).wait_recv()
        pick(f, j, meta_p, rest_p, ((xrows, CAP), (s_x, CAP), (s_y, CAP)))
        dispatch(f, j, 4).start()
        dispatch(f, j, 5).start()
        dispatch(f, j, 1).wait_recv()
        dispatch(f, j, 6).start()

    def load_weights(k):
        @pl.when(k < NC)
        def _():
            w_move(0, k).wait_recv()
            w_move(1, k).wait_recv()

        for cp in w_copies(k):
            cp.start()

    def hidden(k, f, j):
        for i in (2, 3, 4, 5, 6):
            dispatch(f, j, i).wait_recv()
        for cp in w_copies(k):
            cp.wait()

        @pl.when(k < STEPS - 1)
        def _():
            load_weights(k + 1)

        @pl.when(j == 0)
        def _():
            acc[...] = jnp.zeros_like(acc)

        x = xrows[f, :, columns(j)]
        for i in range(4):
            acc[i] += jnp.dot(x, wbuf[lax.rem(k, 2), i], preferred_element_type=F32)

        @pl.when(j == NC - 1)
        def _():
            for i in range(2):
                g = acc[2 * i]
                hid[f, :, i * H : (i + 1) * H] = (g / (1.0 + jnp.exp(-g)) * acc[2 * i + 1]).astype(BF)

    def combine(f, j, i):
        src, dst, mask = (
            lambda: (g_p.at[f, j, pl.ds(0, CAP)], r_p.at[f, j, pl.ds(0, CAP)], PAIR),
            lambda: (g_x.at[f, j], r_x.at[f, j], CROSS),
            lambda: (g_y.at[f, j], r_y.at[f, j], FAR),
            lambda: (g_t.at[f, j], r_t.at[f, j], PAIR),
            lambda: (g_d.at[f, j], r_d.at[f, j], DIAG),
            lambda: (g_p.at[f, j], r_p.at[f, j], PAIR),
            lambda: (g_y.at[f, j, pl.ds(0, CAP)], r_y.at[f, j, pl.ds(0, CAP)], FAR),
        )[i]()
        return remote(src, dst, com_s.at[f, j, i], com_r.at[f, j, i], mask)

    def handoff(f, j):
        section = jnp.where(f == 0, up, down)
        return remote(fin.at[f, j], out.at[f, :, columns(j)], com_s.at[f, j, 7], com_r.at[f, j, 7], 0, section)

    def first_half(f, j):
        section = jnp.where(f == 0, up, down)
        rows = pl.ds(0, CAP)
        return remote(fin.at[f, j, rows], out.at[f, rows, columns(j)], com_s.at[f, j, 7], com_r.at[f, j, 7], 0, section)

    def second_half(f, j):
        return remote(fin.at[f, j, pl.ds(CAP, CAP)], half_way.at[j], way_s.at[j], way_r.at[j], 0, to_relay)

    def relayed(f, j):
        return remote(half_way.at[j], out.at[f, pl.ds(CAP, CAP), columns(j)], way_s.at[j], last_r.at[j], 0, from_relay)

    def hand_over(f, j):
        @pl.when(wraps(f))
        def _():
            first_half(f, j).start()
            second_half(f, j).start()

        @pl.when(jnp.logical_not(wraps(f)))
        def _():
            handoff(f, j).start()

    front_between = (lax.rem(sec, ROW) == 1).astype(jnp.int32)

    def relay(j):
        second_half(front_between, j).wait_recv()
        relayed(front_between, j).start()

    def gated(f, kind, cols, parts):
        z = jnp.concatenate(parts, axis=0)
        high = jnp.dot(gates[f, kind, 0, :, cols], z, preferred_element_type=F32)
        return high + jnp.dot(gates[f, kind, 1, :, cols], z, preferred_element_type=F32)

    def first(m, f, j):
        for cp in d_copies(m):
            cp.wait()

        @pl.when(m < STEPS - 1)
        def _():
            for cp in d_copies(m + 1):
                cp.start()

        q = jnp.dot(hid[f], dbuf[lax.rem(m, 2)], preferred_element_type=F32).astype(BF)
        g_p[f, j, :CAP] = q[7 * CAP :]
        g_p[f, j, CAP:] = q[5 * CAP : 6 * CAP]
        g_x[f, j] = q[2 * CAP : 4 * CAP]
        keep[f, j] = q[6 * CAP : 7 * CAP]
        g_y[f, j] = q[4 * CAP : 6 * CAP]
        @pl.when(summed(f, j))
        def _():
            combine(f, j, 5).start()

        @pl.when(jnp.logical_not(summed(f, j)))
        def _():
            combine(f, j, 0).start()
            combine(f, j, 2).start()

        combine(f, j, 1).start()
        loc[f, j] = q[: 2 * CAP]

    def add(a, b):
        return (a.astype(F32) + b.astype(F32)).astype(BF)

    def second(f, j):
        @pl.when(summed(f, j))
        def _():
            combine(f, j, 5).wait_recv()
            g_d[f, j] = add(keep[f, j], r_p[f, j, :CAP])
            combine(f, j, 4).start()
            g_y[f, j, :CAP] = add(g_y[f, j, :CAP], r_p[f, j, CAP:])
            combine(f, j, 6).start()
            combine(f, j, 1).wait_recv()
            parts = [loc[f, j, CAP:], r_x[f, j, CAP:]]
            g_t[f, j] = gated(f, 0, slice(0, 2 * CAP), parts).astype(BF)

        @pl.when(jnp.logical_not(summed(f, j)))
        def _():
            combine(f, j, 0).wait_recv()
            g_d[f, j] = add(keep[f, j], r_p[f, j, :CAP])
            combine(f, j, 4).start()
            combine(f, j, 1).wait_recv()
            combine(f, j, 2).wait_recv()
            parts = [loc[f, j, CAP:], r_x[f, j, CAP:], r_y[f, j, CAP:]]
            g_t[f, j] = gated(f, 0, slice(0, 3 * CAP), parts).astype(BF)

        combine(f, j, 3).start()

    def third(f, j):
        @pl.when(summed(f, j))
        def _():
            combine(f, j, 6).wait_recv()

        combine(f, j, 4).wait_recv()
        combine(f, j, 3).wait_recv()
        parts = [loc[f, j, :CAP], r_x[f, j, :CAP], r_y[f, j, :CAP], r_d[f, j]]
        total = gated(f, 1, slice(0, 4 * CAP), parts)
        total = total + r_t[f, j].astype(F32) + tokv[f, :, columns(j)].astype(F32)
        fin[f, j] = total.astype(BF)
        hand_over(f, j)

    def at(step, lag, body):
        n = step - lag

        @pl.when((n >= 0) & (n < STEPS))
        def _():
            turn = n // NC
            body(jnp.where(flip == 1, 1 - turn, turn), n - turn * NC)

    meta[...] = jnp.zeros_like(meta)
    for f in range(2):
        meta[f, 0:2, :TOK] = (ids[f] * (CAP + 1) + slots[f]).astype(F32)
        meta[f, 2:4, :TOK] = gate_in[f]
    meta_move.start()
    for f in range(2):
        tok_copy(f).wait()
    send_own(flip, 0)
    for j in range(NC):
        w_move(0, j).start()
        w_move(1, j).start()
    d_move.start()
    meta_move.wait_recv()
    for f in range(2):
        for kind, table in enumerate((meta_p, meta)):
            gates[f, kind, 0], gates[f, kind, 1] = gating(table, f)

    def step(n):
        @pl.when(n > 0)
        def _():
            at(n, 0, send_own)

        at(n, LAG, send_partner)

        @pl.when(n == LATE - 1)
        def _():
            load_weights(0)

        @pl.when(n == STEPS - 1)
        def _():
            d_move.wait_recv()
            for cp in d_copies(0):
                cp.start()

        at(n, STEPS, lambda f, j: first(n - STEPS, f, j))
        at(n, STEPS + SECOND, second)
        at(n, STEPS + THIRD, third)
        at(n, LATE, lambda f, j: hidden(n - LATE, f, j))

        @pl.when(jnp.logical_not(ends) & (n >= STEPS + RELAY) & (n < STEPS + RELAY + NC))
        def _():
            relay(n - STEPS - RELAY)


    each(2 * STEPS + THIRD, step)

    meta_move.wait_send()
    d_move.wait_send()

    def drain_weights(j):
        w_move(0, j).wait_send()
        w_move(1, j).wait_send()

    each(NC, drain_weights)

    def drain(n):
        f = n // NC
        j = n - f * NC
        for i in range(7):
            dispatch(f, j, i).wait_send()
        for i in (1, 3, 4):
            combine(f, j, i).wait_send()

        @pl.when(summed(f, j))
        def _():
            combine(f, j, 5).wait_send()
            combine(f, j, 6).wait_send()

        @pl.when(jnp.logical_not(summed(f, j)))
        def _():
            combine(f, j, 0).wait_send()
            combine(f, j, 2).wait_send()

        @pl.when(wraps(f))
        def _():
            first_half(f, j).wait_send()
            second_half(f, j).wait_send()

        @pl.when(jnp.logical_not(wraps(f)))
        def _():
            handoff(f, j).wait_send()

        @pl.when(arrives(f))
        def _():
            first_half(f, j).wait_recv()
            relayed(f, j).wait_recv()

        @pl.when(jnp.logical_not(arrives(f)))
        def _():
            handoff(f, j).wait_recv()


    each(STEPS, drain)

    @pl.when(jnp.logical_not(ends))
    def _():
        each(NC, lambda j: relayed(front_between, j).wait_send())


def local(tokens, route_ids, slot_index, gate_values, w_gate, w_up, w_down):
    routing = [jnp.swapaxes(x[:, 0], 1, 2) for x in (route_ids, slot_index, gate_values)]
    hbm = pl.BlockSpec(memory_space=pltpu.HBM)
    vmem = pl.BlockSpec(memory_space=pltpu.VMEM)
    dma = pltpu.SemaphoreType.DMA

    def buf(*shape):
        return pltpu.VMEM(shape, BF)

    table = pltpu.VMEM((2, 8, 2 * TOK), F32)
    half = buf(2, NC, CAP, CW)
    whole = buf(2, NC, TOK, CW)
    shapes = ((2, TOK, D), (D, H), (D, H), (H, D))
    out = pl.pallas_call(
        kernel,
        out_shape=[jax.ShapeDtypeStruct(shape, BF) for shape in shapes],
        in_specs=[hbm, vmem, vmem, vmem, hbm, hbm, hbm],
        out_specs=[hbm] * 4,
        scratch_shapes=[
            buf(2, TOK, D), buf(2, TOK, D), buf(2, TOK, D), table, table, buf(2, 2, 2, TOK, 4 * CAP),
            buf(2, 8 * CAP, D), buf(2, 2 * CAP, D), buf(2, 2 * CAP, D), buf(2, CAP, D),
            buf(2, 4, CW, H), buf(2, 2 * H, CW), pltpu.VMEM((4, 8 * CAP, H), F32), buf(2, 8 * CAP, 2 * H),
            whole, whole, whole, whole, half, half, whole,
            whole, whole, whole, half, whole, whole, buf(NC, CAP, CW),
            dma((2,)), dma((2, 4)), dma((2, 2)), dma((NC, 2)), dma((NC, 2)), dma, dma, dma, dma,
            dma((2, NC, 7)), dma((2, NC, 7)), dma((2, NC, 8)), dma((2, NC, 8)), dma((NC,)), dma((NC,)), dma((NC,)),
        ],
        compiler_params=pltpu.CompilerParams(
            collective_id=0, has_side_effects=True, vmem_limit_bytes=63 * 2**20
        ),
        name="relay_layer",
    )(tokens[:, 0], *routing, w_gate[0, 0], w_up[0, 0], w_down[0, 0])
    return out[0][:, None]


def solution(mesh):
    spread = P(None, "section", "expert", None)
    split = P("section", "expert", None, None)
    return jax.shard_map(
        local,
        mesh=mesh,
        in_specs=(spread,) * 4 + (split,) * 3,
        out_specs=spread,
        check_vma=False,
    )
```
